32 devices in a mesh: groups: 2 (over y), inst: 4 (over z), dom: 4 (over x, core).
Axes of the slice: x: 2, y: 2, z: 4, core: 2. Of those that a mesh axis runs over, the one named last changes fastest.
Arguments:
- flow_state: float32 [10, 512, 512], P('groups', 'dom', 'inst'), parts along dimension 0, may hold values from -2 to 3.5, as said below
- op_weight: bfloat16 [9, 320, 320], replicated, may hold values from -0.109375 to 0.109375
- adjacency: int32 [512, 6], P('dom'), may hold values from 0 to 511, as said below
- face_tile: int32 [1024], P('dom'), may hold values from 0 to 511, as said below
- face_row: int32 [1024], P('dom'), may hold values from 0 to 63
- face_partner: int32 [1024], P('dom'), may hold values from 0 to 511
- face_side: int32 [1024], P('dom'), may hold values from 0 to 1
- face_count: int32 [4], P('dom'), may hold values from 64 to 256, as said below
- frequency: float32 [2], P('groups'), parts along dimension 0, may hold values from 0.05 to 0.2
Outputs:
- residual: float32 [10, 512, 512], P('groups', 'dom', 'inst'), parts along dimension 0
The draws below stay inside these ranges and needn't reach their ends.
There are 2 independent parts, one for each index of `groups`. The reference program is written for one: setup_inputs(seed, part) draws one part's arguments, and reference() takes and returns one part's arrays. A program takes and returns all parts, laid end to end along the dimension named above; an argument that names none is the same for every part. Nothing has to cross between parts.
Inputs may be any that keep to these rules, and one draw needn't show every extreme that they name: `flow_state`: density (component 0) lies in [0.5, 2], energy (component 4) in [2, 3.5], momenta in [-2, 2]. `adjacency`: each neighbour lies within 16 tiles of its tile; upper slots point up, lower slots down, clipped at the slab's ends. `face_tile`: row n's tile lies in partition n // 256. `face_count`: at least 64; one partition uses all 256 rows in every draw.
All inputs are finite; a program needn't handle non-finite values.
Results may differ from the reference program's by a relative error of at most 0.0029.
Values may be sent and summed in bfloat16 or wider, within the bound.
A program may use at most 64 MiB of HBM per device.

```python
import math
import jax
import jax.numpy as jnp
from jax import lax

COMPS = 5
TILE_CELLS = 64
BLADES = 4
NEIGHBORS = 6
OPS = 9
RIM = 16
TILES_DEV = 128
FACES_DEV = 256
TILES = 512
INSTANCES = 8
LAG = 2
N_DOM = 4


def draw_flow_state(key, part):
    key = jax.random.fold_in(key, 11)
    keys = jax.random.split(key, 3)
    shape = (TILES, INSTANCES * TILE_CELLS)
    density = jax.random.uniform(keys[0], shape, jnp.float32, 0.6, 1.6)
    momenta = 0.5 * jnp.clip(jax.random.normal(keys[1], (3,) + shape, jnp.float32), -4.0, 4.0)
    energy = jax.random.uniform(keys[2], shape, jnp.float32, 2.0, 3.0)
    return jnp.concatenate([density[None], momenta, energy[None]], axis=0).astype(jnp.float32)


def draw_adjacency(key, part):
    key = jax.random.fold_in(key, 12)
    steps_away = jax.random.randint(key, (TILES, NEIGHBORS), 1, RIM + 1)
    slot_sign = jnp.where(jnp.arange(NEIGHBORS) % 2 == 0, 1, -1).astype(jnp.int32)
    tile_ids = jnp.arange(TILES, dtype=jnp.int32)[:, None]
    return jnp.clip(tile_ids + slot_sign[None, :] * steps_away, 0, TILES - 1).astype(jnp.int32)


def draw_face_tile(key, part):
    key = jax.random.fold_in(key, 13)
    within = jax.random.randint(key, (N_DOM * FACES_DEV,), 0, TILES_DEV)
    partition = jnp.arange(N_DOM * FACES_DEV, dtype=jnp.int32) // FACES_DEV
    return (partition * TILES_DEV + within).astype(jnp.int32)


def draw_face_count(key, part):
    key = jax.random.fold_in(key, 14)
    first_key, second_key = jax.random.split(key)
    counts = jax.random.randint(first_key, (N_DOM,), FACES_DEV // 4, FACES_DEV + 1)
    fullest = jax.random.randint(second_key, (), 0, N_DOM)
    return counts.at[fullest].set(FACES_DEV).astype(jnp.int32)


def place_ends(values, rng, least, high):
    spot = [jax.random.randint(jax.random.fold_in(rng, axis), (), 0, length) for axis, length in enumerate(values.shape)]
    longest = values.shape.index(max(values.shape))
    next_to = spot[:longest] + [(spot[longest] + 1) % values.shape[longest]] + spot[longest + 1:]
    return values.at[tuple(spot)].set(least).at[tuple(next_to)].set(high)


def noise(key, shape, deviation, bound, held_as=jnp.bfloat16):
    entries = jax.random.normal(key, shape, jnp.float32) * deviation
    return jnp.minimum(jnp.maximum(entries, -bound), bound).astype(held_as)


def setup_inputs(seed: int = 0, part: int = 0) -> dict:
    arg_keys = jax.random.split(jax.random.key(seed), 10)
    own_keys = jax.random.split(jax.random.fold_in(arg_keys[9], part), 10)
    flow_state = draw_flow_state(jax.random.fold_in(jax.random.fold_in(arg_keys[9], part), 71), part)
    op_weight = noise(arg_keys[1], (OPS, COMPS * TILE_CELLS, COMPS * TILE_CELLS), (OPS * COMPS * TILE_CELLS) ** -0.5, 0.109375)
    adjacency = draw_adjacency(jax.random.fold_in(arg_keys[9], 71), part)
    face_tile = draw_face_tile(jax.random.fold_in(arg_keys[9], 71), part)
    face_row = place_ends(jax.random.randint(arg_keys[4], (N_DOM * FACES_DEV,), 0, TILE_CELLS), jax.random.fold_in(arg_keys[4], 1), 0, TILE_CELLS - 1).astype(jnp.int32)
    face_partner = place_ends(jax.random.randint(arg_keys[5], (N_DOM * FACES_DEV,), 0, TILES), jax.random.fold_in(arg_keys[5], 1), 0, TILES - 1).astype(jnp.int32)
    face_side = place_ends(jax.random.randint(arg_keys[6], (N_DOM * FACES_DEV,), 0, 2), jax.random.fold_in(arg_keys[6], 1), 0, 1).astype(jnp.int32)
    face_count = draw_face_count(jax.random.fold_in(arg_keys[9], 71), part)
    frequency = jnp.clip(jnp.exp(jax.random.uniform(own_keys[8], (1,), jnp.float32, math.log(0.05), math.log(0.2))), 0.05, 0.2)
    return {"flow_state": flow_state, "op_weight": op_weight, "adjacency": adjacency, "face_tile": face_tile, "face_row": face_row, "face_partner": face_partner, "face_side": face_side, "face_count": face_count, "frequency": frequency}


def flux_stack(values):
    density = values[0]
    safe_density = jnp.where(density > 0, density, 1.0)
    momenta = values[1:4]
    energy = values[4]
    speeds = momenta / safe_density
    pressure = 0.4 * (energy - 0.5 * jnp.sum(momenta * speeds, axis=0))
    result = []
    for direction in range(3):
        normal_speed = speeds[direction]
        pieces = [momenta[direction]]
        for component in range(3):
            product_term = momenta[component] * normal_speed
            if component == direction:
                product_term = product_term + pressure
            pieces.append(product_term)
        pieces.append((energy + pressure) * normal_speed)
        result.append(jnp.stack(pieces))
    return jnp.stack(result).astype(jnp.bfloat16)


def spectral_matrix(instances):
    positions = jnp.arange(instances, dtype=jnp.int32)
    offsets = positions[:, None] - positions[None, :]
    parity = 1.0 - 2.0 * (offsets % 2).astype(jnp.float32)
    angles = offsets.astype(jnp.float32) * (math.pi / instances)
    safe_angles = jnp.where(offsets == 0, 1.0, angles)
    return jnp.where(offsets == 0, 0.0, 0.5 * parity / jnp.tan(safe_angles)).astype(jnp.float32)


def rotate_momenta(values, cosine, sine_turn):
    rotated_x = cosine * values[1] - sine_turn * values[2]
    rotated_y = sine_turn * values[1] + cosine * values[2]
    return jnp.stack([values[0], rotated_x, rotated_y, values[3], values[4]])


def reference(flow_state, op_weight, adjacency, face_tile, face_row, face_partner, face_side, face_count, frequency):
    row_width = INSTANCES * TILE_CELLS
    grid = flow_state.reshape(COMPS, TILES, INSTANCES, TILE_CELLS)
    weights = op_weight.astype(jnp.float32).reshape(OPS, COMPS, TILE_CELLS, COMPS, TILE_CELLS)
    per_instance = jnp.moveaxis(grid, 2, 0)

    def one_instance(values):
        fluxes = flux_stack(values).astype(jnp.float32)
        accumulated = jnp.zeros((COMPS, TILES, TILE_CELLS), jnp.float32)
        for neighbor in range(NEIGHBORS):
            picked = jnp.take(fluxes[neighbor // 2], adjacency[:, neighbor], axis=1)
            accumulated = accumulated + jnp.einsum("ctx,cxey->ety", picked, weights[neighbor])
        for direction in range(3):
            accumulated = accumulated + jnp.einsum("ctx,cxey->ety", fluxes[direction], weights[NEIGHBORS + direction])
        return accumulated

    spatial = jnp.moveaxis(lax.map(one_instance, per_instance), 0, 2)
    spectral = spectral_matrix(INSTANCES)
    temporal = frequency[0] * jnp.einsum("kj,ctjx->ctkx", spectral, grid, precision=lax.Precision.HIGHEST)
    accumulated = (spatial + temporal).reshape(COMPS, TILES * row_width)

    faces_total = N_DOM * FACES_DEV
    slot_ids = jnp.arange(faces_total, dtype=jnp.int32)
    partition = slot_ids // FACES_DEV
    live_mask = ((slot_ids % FACES_DEV) < face_count[partition]).astype(jnp.float32)
    inst_ids = jnp.arange(INSTANCES, dtype=jnp.int32)
    upper_ids = (inst_ids + LAG) % INSTANCES
    lower_ids = (inst_ids - LAG) % INSTANCES
    lag_ids = jnp.where(face_side[:, None] == 1, upper_ids[None, :], lower_ids[None, :]).astype(jnp.int32)
    partner_pos = (face_partner[:, None] * row_width + lag_ids * TILE_CELLS + face_row[:, None]).astype(jnp.int32)
    own_pos = (face_tile[:, None] * row_width + inst_ids[None, :] * TILE_CELLS + face_row[:, None]).astype(jnp.int32)
    flat_state = flow_state.reshape(COMPS, TILES * row_width)
    lagged = flat_state[:, partner_pos]
    own_vals = flat_state[:, own_pos]
    sine_turn = (jnp.where(face_side == 1, 1.0, -1.0) * math.sin(2.0 * math.pi / BLADES)).astype(jnp.float32)[:, None]
    cosine = math.cos(2.0 * math.pi / BLADES)
    rotated = rotate_momenta(lagged, cosine, sine_turn)
    change = live_mask[None, :, None] * (rotated - own_vals)
    accumulated = accumulated.at[:, own_pos].add(change)
    return accumulated.reshape(COMPS, TILES, row_width)
```

```python
import functools
import math

import jax
import jax.numpy as jnp
from jax import lax
from jax.experimental import pallas as pl
from jax.experimental.pallas import tpu as pltpu
from jax.sharding import PartitionSpec as P

BLADES = 4
NEIGHBORS = 6
RIM = 16
MESH = pl.DeviceIdType.MESH
CHUNK = 16


def derivative_entry(offset, instances):
    offset %= instances
    if offset == 0 or 2 * offset == instances:
        return 0.0
    return 0.5 * (-1.0) ** offset / math.tan(math.pi * offset / instances)


def fluxes(values):
    density = values[0]
    safe_density = jnp.where(density > 0, density, 1.0)
    momenta = values[1:4]
    energy = values[4]
    speeds = [m / safe_density for m in momenta]
    kinetic = momenta[0] * speeds[0] + momenta[1] * speeds[1] + momenta[2] * speeds[2]
    pressure = 0.4 * (energy - 0.5 * kinetic)
    result = []
    for direction in range(3):
        pieces = [momenta[direction]]
        for component in range(3):
            term = momenta[component] * speeds[direction]
            pieces.append(term + pressure if component == direction else term)
        pieces.append((energy + pressure) * speeds[direction])
        result.append(pieces)
    return result


def kernel(
    peers_inst, peers_dom, cells,
    flow, weight, adj, face_tile, face_row, face_partner, face_side, count, freq,
    out,
    ubf, ain, tout, tin, stage, halo, wv, fp, ut, codes, pout, pin, acc,
    w_sem, code_sem, halo_sem, a_sem, t_sem, p_sem,
):
    n, ndom = peers_inst, peers_dom
    comps, tiles, width = flow.shape
    faces = face_tile.shape[1]
    slots = width // cells
    instances = n * slots
    lag = instances // BLADES // slots
    part = tiles // n
    ops = weight.shape[0]
    per_op = comps * cells
    aligned = part % CHUNK == 0
    rows = ubf.shape[1]
    wide = fp.shape[2] // slots
    shift = cells.bit_length() - 1
    me_i = lax.axis_index("inst")
    me_d = lax.axis_index("dom")

    def inst_at(step):
        return lax.rem(me_i + (step % n), n)

    def dom_at(step):
        return lax.rem(me_d + (step % ndom), ndom)

    def at(dom_step, inst_step):
        return {"inst": inst_at(inst_step), "dom": dom_at(dom_step)}

    def remote(src, dst, sems, index, target):
        return pltpu.make_async_remote_copy(
            src_ref=src,
            dst_ref=dst,
            send_sem=sems.at[(0,) + index],
            recv_sem=sems.at[(1,) + index],
            device_id=target,
            device_id_type=MESH,
        )

    partners = {(j, 0) for j in range(1, ndom)} | {(0, i) for i in range(1, n)}
    partners |= {(j, s % n) for j in range(ndom) for s in (lag, -lag)}
    partners = sorted(partners)
    barrier = pltpu.get_barrier_semaphore()
    for dom_step, inst_step in partners:
        pl.semaphore_signal(
            barrier, inc=1, device_id=at(dom_step, inst_step), device_id_type=MESH
        )
    weights_in = pltpu.make_async_copy(weight, wv, w_sem)
    weights_in.start()

    code = face_partner[...] * cells + face_row[...]
    codes[0] = jnp.broadcast_to(code, (8, faces))
    for p in range(n):
        if aligned:
            for c in range(comps):
                ubf[p, c * part : (c + 1) * part] = flow[
                    c, p * part : (p + 1) * part
                ].astype(jnp.bfloat16)
        else:
            stage[...] = jnp.zeros_like(stage)
            for c in range(comps):
                stage[c * part : (c + 1) * part] = flow[c, p * part : (p + 1) * part]
            ubf[p] = stage[...].astype(jnp.bfloat16)
    pl.semaphore_wait(barrier, len(partners))

    code_copies = [
        remote(codes.at[0], codes.at[j], code_sem, (j,), at(j, 0)) for j in range(1, ndom)
    ]
    for copy in code_copies:
        copy.start()
    a_copies = [
        remote(ubf.at[inst_at(i)], ain.at[i], a_sem, (i,), at(0, i)) for i in range(1, n)
    ]
    for copy in a_copies:
        copy.start()
    halo_copies = [
        remote(flow.at[:, tiles - RIM :], halo.at[0], halo_sem, (0,), at(1, 0)),
        remote(flow.at[:, :RIM], halo.at[1], halo_sem, (1,), at(-1, 0)),
    ]
    for copy in halo_copies:
        copy.start()

    low_lanes = lax.broadcasted_iota(jnp.int32, (CHUNK, width), 1) < cells

    def swap(value):
        return pltpu.roll(value, cells, 1)

    def put_fluxes(read, base):
        for direction, pieces in enumerate(fluxes(read)):
            for pair in range((comps + 1) // 2):
                first = pieces[2 * pair]
                cols = slice(pair * width, (pair + 1) * width)
                more = slice(wide + pair * width, wide + (pair + 1) * width)
                if 2 * pair + 1 < comps:
                    second = pieces[2 * pair + 1]
                    left = jnp.where(low_lanes, first, swap(second))
                    right = jnp.where(low_lanes, swap(first), second)
                else:
                    left, right = first, swap(first)
                fp[direction, base : base + CHUNK, cols] = left.astype(jnp.bfloat16)
                fp[direction, base : base + CHUNK, more] = right.astype(jnp.bfloat16)

    for c in range(comps):
        ut[c * width : (c + 1) * width] = flow[c].T.astype(jnp.bfloat16)
    for t in range(0, tiles, CHUNK):
        put_fluxes([flow[c, t : t + CHUNK] for c in range(comps)], RIM + t)

    cell_ids = lax.broadcasted_iota(jnp.int32, (cells, faces), 0)
    tile_ids = lax.broadcasted_iota(jnp.int32, (tiles, faces), 0)
    p_copies = []
    for j in range(ndom):
        if j:
            code_copies[j - 1].wait_recv()
        wanted = codes[j][:1]
        wanted_tile = lax.shift_right_logical(wanted, shift) - me_d * tiles
        wanted_cell = lax.bitwise_and(wanted, cells - 1)
        pick = jnp.where(tile_ids == wanted_tile, 1.0, 0.0).astype(jnp.bfloat16)
        found = jnp.dot(ut[...], pick, preferred_element_type=jnp.float32)
        mask = cell_ids == wanted_cell
        lines = [
            jnp.sum(
                jnp.where(mask, found[g * cells : (g + 1) * cells], 0.0),
                axis=0,
                keepdims=True,
            )
            for g in range(comps * slots)
        ]
        lines.append(jnp.zeros((pout.shape[1] - comps * slots, faces), jnp.float32))
        pout[j] = jnp.concatenate(lines, axis=0).astype(jnp.bfloat16)
        for way, step in enumerate((-lag, lag)):
            copy = remote(pout.at[j], pin.at[way, j], p_sem, (way, j), at(-j, step))
            copy.start()
            p_copies.append(copy)

    for copy in a_copies:
        copy.wait_recv()
    cross = [
        jnp.where(
            low_lanes,
            derivative_entry(2 * delta - 1, instances),
            derivative_entry(2 * delta + 1, instances),
        ).astype(jnp.float32)
        for delta in range(n)
    ]
    for r in range(0, rows, CHUNK):
        plain = [
            (ubf[me_i, r : r + CHUNK] if i == 0 else ain[i, r : r + CHUNK]).astype(jnp.float32)
            for i in range(n)
        ]
        turned = [swap(value) for value in plain]
        for m in range(n):
            total = jnp.zeros((CHUNK, width), jnp.float32)
            for i in range(n):
                even = derivative_entry(2 * (m + i), instances)
                if even != 0.0:
                    total = total + even * plain[i]
                total = total + cross[(m + i) % n] * turned[i]
            total = total.astype(jnp.bfloat16)
            if m == 0:
                tin[me_i, r : r + CHUNK] = total
            else:
                tout[m, r : r + CHUNK] = total
    t_copies = [
        remote(tout.at[m], tin.at[me_i], t_sem, (m,), at(0, m)) for m in range(1, n)
    ]
    for copy in t_copies:
        copy.start()

    weights_in.wait()

    def apply(left, right, op):
        w = wv[op]
        both = jnp.concatenate([left, right], axis=0)
        return jnp.dot(both, w, preferred_element_type=jnp.float32)

    total = None
    for direction in range(3):
        own = fp[direction, RIM : RIM + tiles]
        term = apply(own[:, :per_op], own[:, wide : wide + per_op], NEIGHBORS + direction)
        total = term if total is None else total + term

    for copy in halo_copies:
        copy.wait_recv()
    for side, base in ((0, 0), (1, RIM + tiles)):
        put_fluxes([halo[side, c] for c in range(comps)], base)
    neighbor_ids = lax.broadcasted_iota(jnp.int32, (tiles, tiles + 2 * RIM), 1)
    shifted = adj[...] - (me_d * tiles - RIM)
    for direction in range(3):
        pick = jnp.concatenate(
            [
                jnp.where(shifted[:, s : s + 1] == neighbor_ids, 1.0, 0.0).astype(jnp.bfloat16)
                for s in (2 * direction, 2 * direction + 1)
            ],
            axis=0,
        )
        picked = jnp.dot(pick, fp[direction], preferred_element_type=jnp.float32)
        picked = picked.astype(jnp.bfloat16)
        for s in range(2):
            block = picked[s * tiles : (s + 1) * tiles]
            total = total + apply(
                block[:, :per_op], block[:, wide : wide + per_op], 2 * direction + s
            )
    acc[:, :per_op] = total

    side = face_side[...] == 1
    live = lax.broadcasted_iota(jnp.int32, (1, faces), 1) < count[0]
    own_tile = jnp.where(live, face_tile[...] - me_d * tiles, -1)
    place = jnp.where(tile_ids == own_tile, 1.0, 0.0).astype(jnp.bfloat16)
    mask = cell_ids == face_row[...]
    ones = jnp.where(mask, 1.0, 0.0).astype(jnp.bfloat16)
    contract = (((1,), (1,)), ((), ()))
    times = lax.dot_general(
        place, jnp.concatenate([ones] * slots, axis=0), contract,
        preferred_element_type=jnp.float32,
    )
    for copy in p_copies:
        copy.wait_recv()
    upper = pin[0, 0].astype(jnp.float32)
    lower = pin[1, 0].astype(jnp.float32)
    for j in range(1, ndom):
        upper = upper + pin[0, j].astype(jnp.float32)
        lower = lower + pin[1, j].astype(jnp.float32)
    lagged = jnp.where(side, upper, lower)
    lines = [lagged[g : g + 1] for g in range(comps * slots)]
    cosine = math.cos(2.0 * math.pi / BLADES)
    sine = jnp.where(side, 1.0, -1.0) * math.sin(2.0 * math.pi / BLADES)
    for k in range(slots):
        m0, m1 = lines[slots + k], lines[2 * slots + k]
        lines[slots + k] = cosine * m0 - sine * m1
        lines[2 * slots + k] = sine * m0 + cosine * m1
    spread = jnp.concatenate(
        [jnp.where(mask, line, 0.0).astype(jnp.bfloat16) for line in lines], axis=0
    )
    gained = lax.dot_general(place, spread, contract, preferred_element_type=jnp.float32)

    for copy in t_copies:
        copy.wait_recv()
    speed = freq[0]
    low = lax.broadcasted_iota(jnp.int32, (part, width), 1) < cells
    for p in range(n):
        span = slice(p * part, (p + 1) * part)
        more = slice(tiles + p * part, tiles + (p + 1) * part)
        if not aligned:
            stage[...] = tin[p].astype(jnp.float32)
        for c in range(comps):
            pair = c // 2
            cols = slice(pair * width, (pair + 1) * width)
            if c % 2 == 0:
                spatial = jnp.where(low, acc[span, cols], swap(acc[more, cols]))
            else:
                spatial = jnp.where(low, swap(acc[span, cols]), acc[more, cols])
            block = slice(c * part, (c + 1) * part)
            temporal = tin[p, block].astype(jnp.float32) if aligned else stage[block]
            out[c, span] = (
                spatial
                + speed * temporal
                + gained[span, c * width : (c + 1) * width]
                - times[span] * flow[c, span]
            )

    for copy in code_copies + a_copies + halo_copies + p_copies + t_copies:
        copy.wait_send()


def body(
    n, ndom,
    flow_state, op_weight, adjacency, face_tile, face_row, face_partner, face_side,
    face_count, frequency,
):
    comps, tiles, width = flow_state.shape
    ops, per_op, _ = op_weight.shape
    cells = per_op // comps
    faces = face_tile.shape[0]
    slots = width // cells
    rows = -(-(comps * (tiles // n)) // CHUNK) * CHUNK
    wide = -(-comps // 2) * width
    packed = -(-(comps * slots) // 16) * 16
    in_vmem = pl.BlockSpec(memory_space=pltpu.VMEM)
    in_smem = pl.BlockSpec(memory_space=pltpu.SMEM)
    bf16, f32 = jnp.bfloat16, jnp.float32
    dma = pltpu.SemaphoreType.DMA
    line = lambda values: values.reshape(1, faces)
    return pl.pallas_call(
        functools.partial(kernel, n, ndom, cells),
        out_shape=jax.ShapeDtypeStruct(flow_state.shape, f32),
        in_specs=[in_vmem, pl.BlockSpec(memory_space=pl.ANY)] + [in_vmem] * 5 + [in_smem] * 2,
        out_specs=in_vmem,
        scratch_shapes=[
            pltpu.VMEM((n, rows, width), bf16),
            pltpu.VMEM((n, rows, width), bf16),
            pltpu.VMEM((n, rows, width), bf16),
            pltpu.VMEM((n, rows, width), bf16),
            pltpu.VMEM((rows, width), f32),
            pltpu.VMEM((2, comps, RIM, width), f32),
            pltpu.VMEM(op_weight.shape, bf16),
            pltpu.VMEM((3, tiles + 2 * RIM, slots * wide), bf16),
            pltpu.VMEM((comps * width, tiles), bf16),
            pltpu.VMEM((ndom, 8, faces), jnp.int32),
            pltpu.VMEM((ndom, packed, faces), bf16),
            pltpu.VMEM((2, ndom, packed, faces), bf16),
            pltpu.VMEM((slots * tiles, wide), f32),
            dma,
            dma((2, ndom)),
            dma((2, 2)),
            dma((2, n)),
            dma((2, n)),
            dma((2, 2, ndom)),
        ],
        compiler_params=pltpu.CompilerParams(
            collective_id=0, has_side_effects=True, vmem_limit_bytes=40 * 1024 * 1024
        ),
    )(
        flow_state, op_weight, adjacency, line(face_tile), line(face_row),
        line(face_partner), line(face_side), face_count, frequency,
    )


def solution(mesh):
    placed = (
        P("groups", "dom", "inst"),
        P(),
        P("dom", None),
        P("dom"),
        P("dom"),
        P("dom"),
        P("dom"),
        P("dom"),
        P("groups"),
    )
    return jax.shard_map(
        functools.partial(body, mesh.shape["inst"], mesh.shape["dom"]),
        mesh=mesh,
        in_specs=placed,
        out_specs=P("groups", "dom", "inst"),
        check_vma=False,
    )
```

```python
import functools
import math

import jax
import jax.numpy as jnp
from jax import lax
from jax.experimental import pallas as pl
from jax.experimental.pallas import tpu as pltpu
from jax.sharding import PartitionSpec as P

BLADES = 4
NEIGHBORS = 6
RIM = 16
MESH = pl.DeviceIdType.MESH
CHUNK = 16


def derivative_entry(offset, instances):
    offset %= instances
    if offset == 0 or 2 * offset == instances:
        return 0.0
    return 0.5 * (-1.0) ** offset / math.tan(math.pi * offset / instances)


def fluxes(values):
    density = values[0]
    safe_density = jnp.where(density > 0, density, 1.0)
    momenta = values[1:4]
    energy = values[4]
    speeds = [m / safe_density for m in momenta]
    kinetic = momenta[0] * speeds[0] + momenta[1] * speeds[1] + momenta[2] * speeds[2]
    pressure = 0.4 * (energy - 0.5 * kinetic)
    result = []
    for direction in range(3):
        pieces = [momenta[direction]]
        for component in range(3):
            term = momenta[component] * speeds[direction]
            pieces.append(term + pressure if component == direction else term)
        pieces.append((energy + pressure) * speeds[direction])
        result.append(pieces)
    return result


def kernel(
    peers_inst, peers_dom, cells,
    flow_in, weight, adj_in, tile_in, row_in, partner_in, side_in, count_in, freq_in,
    out,
    flow, adj, face_tile, face_row, face_partner, face_side, count, freq,
    ubf, ain, tout, tin, stage, halo, wv, fp, ut, codes, pout, pin, acc,
    in_sem, code_sem, halo_sem, a_sem, t_sem, p_sem,
):
    n, ndom = peers_inst, peers_dom
    comps, tiles, width = flow.shape
    faces = face_tile.shape[1]
    slots = width // cells
    instances = n * slots
    lag = instances // BLADES // slots
    part = tiles // n
    ops = weight.shape[0]
    per_op = comps * cells
    aligned = part % CHUNK == 0
    rows = ubf.shape[1]
    wide = fp.shape[2] // slots
    shift = cells.bit_length() - 1
    me_i = lax.axis_index("inst")
    me_d = lax.axis_index("dom")

    def inst_at(step):
        return lax.rem(me_i + (step % n), n)

    def dom_at(step):
        return lax.rem(me_d + (step % ndom), ndom)

    def at(dom_step, inst_step):
        return {"inst": inst_at(inst_step), "dom": dom_at(dom_step)}

    def remote(src, dst, sems, index, target):
        return pltpu.make_async_remote_copy(
            src_ref=src,
            dst_ref=dst,
            send_sem=sems.at[(0,) + index],
            recv_sem=sems.at[(1,) + index],
            device_id=target,
            device_id_type=MESH,
        )

    partners = {(j, 0) for j in range(1, ndom)} | {(0, i) for i in range(1, n)}
    partners |= {(j, s % n) for j in range(ndom) for s in (lag, -lag)}
    partners = sorted(partners)
    barrier = pltpu.get_barrier_semaphore()
    for dom_step, inst_step in partners:
        pl.semaphore_signal(
            barrier, inc=1, device_id=at(dom_step, inst_step), device_id_type=MESH
        )
    arriving = [
        pltpu.make_async_copy(src, dst, in_sem.at[i])
        for i, (src, dst) in enumerate(
            (
                (flow_in, flow),
                (partner_in, face_partner),
                (row_in, face_row),
                (adj_in, adj),
                (tile_in, face_tile),
                (side_in, face_side),
                (count_in, count),
                (freq_in, freq),
                (weight, wv),
            )
        )
    ]
    for copy in arriving:
        copy.start()
    flow_copy, partner_copy, row_copy, *other_copies, weight_copy = arriving

    partner_copy.wait()
    row_copy.wait()
    code = face_partner[...] * cells + face_row[...]
    codes[0] = jnp.broadcast_to(code, (8, faces))
    flow_copy.wait()
    for p in range(n):
        if aligned:
            for c in range(comps):
                ubf[p, c * part : (c + 1) * part] = flow[
                    c, p * part : (p + 1) * part
                ].astype(jnp.bfloat16)
        else:
            stage[...] = jnp.zeros_like(stage)
            for c in range(comps):
                stage[c * part : (c + 1) * part] = flow[c, p * part : (p + 1) * part]
            ubf[p] = stage[...].astype(jnp.bfloat16)
    pl.semaphore_wait(barrier, len(partners))

    code_copies = [
        remote(codes.at[0], codes.at[j], code_sem, (j,), at(j, 0)) for j in range(1, ndom)
    ]
    for copy in code_copies:
        copy.start()
    a_copies = [
        remote(ubf.at[inst_at(i)], ain.at[i], a_sem, (i,), at(0, i)) for i in range(1, n)
    ]
    for copy in a_copies:
        copy.start()
    halo_copies = [
        remote(flow_in.at[:, tiles - RIM :], halo.at[0], halo_sem, (0,), at(1, 0)),
        remote(flow_in.at[:, :RIM], halo.at[1], halo_sem, (1,), at(-1, 0)),
    ]
    for copy in halo_copies:
        copy.start()

    low_lanes = lax.broadcasted_iota(jnp.int32, (CHUNK, width), 1) < cells

    def swap(value):
        return pltpu.roll(value, cells, 1)

    def put_fluxes(read, base):
        for direction, pieces in enumerate(fluxes(read)):
            for pair in range((comps + 1) // 2):
                first = pieces[2 * pair]
                cols = slice(pair * width, (pair + 1) * width)
                more = slice(wide + pair * width, wide + (pair + 1) * width)
                if 2 * pair + 1 < comps:
                    second = pieces[2 * pair + 1]
                    left = jnp.where(low_lanes, first, swap(second))
                    right = jnp.where(low_lanes, swap(first), second)
                else:
                    left, right = first, swap(first)
                fp[direction, base : base + CHUNK, cols] = left.astype(jnp.bfloat16)
                fp[direction, base : base + CHUNK, more] = right.astype(jnp.bfloat16)

    for c in range(comps):
        ut[c * width : (c + 1) * width] = flow[c].T.astype(jnp.bfloat16)
    for t in range(0, tiles, CHUNK):
        put_fluxes([flow[c, t : t + CHUNK] for c in range(comps)], RIM + t)

    cell_ids = lax.broadcasted_iota(jnp.int32, (cells, faces), 0)
    tile_ids = lax.broadcasted_iota(jnp.int32, (tiles, faces), 0)
    p_copies = []
    for j in range(ndom):
        if j:
            code_copies[j - 1].wait_recv()
        wanted = codes[j][:1]
        wanted_tile = lax.shift_right_logical(wanted, shift) - me_d * tiles
        wanted_cell = lax.bitwise_and(wanted, cells - 1)
        pick = jnp.where(tile_ids == wanted_tile, 1.0, 0.0).astype(jnp.bfloat16)
        found = jnp.dot(ut[...], pick, preferred_element_type=jnp.float32)
        mask = cell_ids == wanted_cell
        lines = [
            jnp.sum(
                jnp.where(mask, found[g * cells : (g + 1) * cells], 0.0),
                axis=0,
                keepdims=True,
            )
            for g in range(comps * slots)
        ]
        lines.append(jnp.zeros((pout.shape[1] - comps * slots, faces), jnp.float32))
        pout[j] = jnp.concatenate(lines, axis=0).astype(jnp.bfloat16)
        for way, step in enumerate((-lag, lag)):
            copy = remote(pout.at[j], pin.at[way, j], p_sem, (way, j), at(-j, step))
            copy.start()
            p_copies.append(copy)

    for copy in a_copies:
        copy.wait_recv()
    cross = [
        jnp.where(
            low_lanes,
            derivative_entry(2 * delta - 1, instances),
            derivative_entry(2 * delta + 1, instances),
        ).astype(jnp.float32)
        for delta in range(n)
    ]
    for r in range(0, rows, CHUNK):
        plain = [
            (ubf[me_i, r : r + CHUNK] if i == 0 else ain[i, r : r + CHUNK]).astype(jnp.float32)
            for i in range(n)
        ]
        turned = [swap(value) for value in plain]
        for m in range(n):
            total = jnp.zeros((CHUNK, width), jnp.float32)
            for i in range(n):
                even = derivative_entry(2 * (m + i), instances)
                if even != 0.0:
                    total = total + even * plain[i]
                total = total + cross[(m + i) % n] * turned[i]
            total = total.astype(jnp.bfloat16)
            if m == 0:
                tin[me_i, r : r + CHUNK] = total
            else:
                tout[m, r : r + CHUNK] = total
    t_copies = [
        remote(tout.at[m], tin.at[me_i], t_sem, (m,), at(0, m)) for m in range(1, n)
    ]
    for copy in t_copies:
        copy.start()

    for copy in other_copies:
        copy.wait()
    weight_copy.wait()

    def apply(left, right, op):
        w = wv[op]
        both = jnp.concatenate([left, right], axis=0)
        return jnp.dot(both, w, preferred_element_type=jnp.float32)

    total = None
    for direction in range(3):
        own = fp[direction, RIM : RIM + tiles]
        term = apply(own[:, :per_op], own[:, wide : wide + per_op], NEIGHBORS + direction)
        total = term if total is None else total + term

    for copy in halo_copies:
        copy.wait_recv()
    for side, base in ((0, 0), (1, RIM + tiles)):
        put_fluxes([halo[side, c] for c in range(comps)], base)
    neighbor_ids = lax.broadcasted_iota(jnp.int32, (tiles, tiles + 2 * RIM), 1)
    shifted = jnp.concatenate([adj[...], jnp.zeros((8 - NEIGHBORS, tiles), jnp.int32)], axis=0)
    shifted = shifted.T - (me_d * tiles - RIM)
    for direction in range(3):
        pick = jnp.concatenate(
            [
                jnp.where(shifted[:, s : s + 1] == neighbor_ids, 1.0, 0.0).astype(jnp.bfloat16)
                for s in (2 * direction, 2 * direction + 1)
            ],
            axis=0,
        )
        picked = jnp.dot(pick, fp[direction], preferred_element_type=jnp.float32)
        picked = picked.astype(jnp.bfloat16)
        for s in range(2):
            block = picked[s * tiles : (s + 1) * tiles]
            total = total + apply(
                block[:, :per_op], block[:, wide : wide + per_op], 2 * direction + s
            )
    acc[:, :per_op] = total

    side = face_side[...] == 1
    live = lax.broadcasted_iota(jnp.int32, (1, faces), 1) < count[0]
    own_tile = jnp.where(live, face_tile[...] - me_d * tiles, -1)
    place = jnp.where(tile_ids == own_tile, 1.0, 0.0).astype(jnp.bfloat16)
    mask = cell_ids == face_row[...]
    ones = jnp.where(mask, 1.0, 0.0).astype(jnp.bfloat16)
    contract = (((1,), (1,)), ((), ()))
    times = lax.dot_general(
        place, jnp.concatenate([ones] * slots, axis=0), contract,
        preferred_element_type=jnp.float32,
    )
    for copy in p_copies:
        copy.wait_recv()
    upper = pin[0, 0].astype(jnp.float32)
    lower = pin[1, 0].astype(jnp.float32)
    for j in range(1, ndom):
        upper = upper + pin[0, j].astype(jnp.float32)
        lower = lower + pin[1, j].astype(jnp.float32)
    lagged = jnp.where(side, upper, lower)
    lines = [lagged[g : g + 1] for g in range(comps * slots)]
    cosine = math.cos(2.0 * math.pi / BLADES)
    sine = jnp.where(side, 1.0, -1.0) * math.sin(2.0 * math.pi / BLADES)
    for k in range(slots):
        m0, m1 = lines[slots + k], lines[2 * slots + k]
        lines[slots + k] = cosine * m0 - sine * m1
        lines[2 * slots + k] = sine * m0 + cosine * m1
    spread = jnp.concatenate(
        [jnp.where(mask, line, 0.0).astype(jnp.bfloat16) for line in lines], axis=0
    )
    gained = lax.dot_general(place, spread, contract, preferred_element_type=jnp.float32)

    for copy in t_copies:
        copy.wait_recv()
    speed = freq[0]
    low = lax.broadcasted_iota(jnp.int32, (part, width), 1) < cells
    for p in range(n):
        span = slice(p * part, (p + 1) * part)
        more = slice(tiles + p * part, tiles + (p + 1) * part)
        if not aligned:
            stage[...] = tin[p].astype(jnp.float32)
        for c in range(comps):
            pair = c // 2
            cols = slice(pair * width, (pair + 1) * width)
            if c % 2 == 0:
                spatial = jnp.where(low, acc[span, cols], swap(acc[more, cols]))
            else:
                spatial = jnp.where(low, swap(acc[span, cols]), acc[more, cols])
            block = slice(c * part, (c + 1) * part)
            temporal = tin[p, block].astype(jnp.float32) if aligned else stage[block]
            out[c, span] = (
                spatial
                + speed * temporal
                + gained[span, c * width : (c + 1) * width]
                - times[span] * flow[c, span]
            )

    for copy in code_copies + a_copies + halo_copies + p_copies + t_copies:
        copy.wait_send()


def body(
    n, ndom,
    flow_state, op_weight, adjacency, face_tile, face_row, face_partner, face_side,
    face_count, frequency,
):
    comps, tiles, width = flow_state.shape
    ops, per_op, _ = op_weight.shape
    cells = per_op // comps
    faces = face_tile.shape[0]
    slots = width // cells
    rows = -(-(comps * (tiles // n)) // CHUNK) * CHUNK
    wide = -(-comps // 2) * width
    packed = -(-(comps * slots) // 16) * 16
    in_vmem = pl.BlockSpec(memory_space=pltpu.VMEM)
    in_hbm = pl.BlockSpec(memory_space=pltpu.HBM)
    i32 = jnp.int32
    bf16, f32 = jnp.bfloat16, jnp.float32
    dma = pltpu.SemaphoreType.DMA
    line = lambda values: values.reshape(1, faces)
    return pl.pallas_call(
        functools.partial(kernel, n, ndom, cells),
        out_shape=jax.ShapeDtypeStruct(flow_state.shape, f32),
        in_specs=[in_hbm] * 9,
        out_specs=in_vmem,
        scratch_shapes=[
            pltpu.VMEM(flow_state.shape, f32),
            pltpu.VMEM((NEIGHBORS, tiles), i32),
            pltpu.VMEM((1, faces), i32),
            pltpu.VMEM((1, faces), i32),
            pltpu.VMEM((1, faces), i32),
            pltpu.VMEM((1, faces), i32),
            pltpu.SMEM((1,), i32),
            pltpu.SMEM((1,), f32),
            pltpu.VMEM((n, rows, width), bf16),
            pltpu.VMEM((n, rows, width), bf16),
            pltpu.VMEM((n, rows, width), bf16),
            pltpu.VMEM((n, rows, width), bf16),
            pltpu.VMEM((rows, width), f32),
            pltpu.VMEM((2, comps, RIM, width), f32),
            pltpu.VMEM(op_weight.shape, bf16),
            pltpu.VMEM((3, tiles + 2 * RIM, slots * wide), bf16),
            pltpu.VMEM((comps * width, tiles), bf16),
            pltpu.VMEM((ndom, 8, faces), jnp.int32),
            pltpu.VMEM((ndom, packed, faces), bf16),
            pltpu.VMEM((2, ndom, packed, faces), bf16),
            pltpu.VMEM((slots * tiles, wide), f32),
            dma((9,)),
            dma((2, ndom)),
            dma((2, 2)),
            dma((2, n)),
            dma((2, n)),
            dma((2, 2, ndom)),
        ],
        compiler_params=pltpu.CompilerParams(
            collective_id=0, has_side_effects=True, vmem_limit_bytes=64 * 1024 * 1024
        ),
    )(
        flow_state, op_weight, adjacency.T, line(face_tile), line(face_row),
        line(face_partner), line(face_side), face_count, frequency,
    )


def solution(mesh):
    placed = (
        P("groups", "dom", "inst"),
        P(),
        P("dom", None),
        P("dom"),
        P("dom"),
        P("dom"),
        P("dom"),
        P("dom"),
        P("groups"),
    )
    return jax.shard_map(
        functools.partial(body, mesh.shape["inst"], mesh.shape["dom"]),
        mesh=mesh,
        in_specs=placed,
        out_specs=P("groups", "dom", "inst"),
        check_vma=False,
    )
```

```python
import functools
import math

import jax
import jax.numpy as jnp
from jax import lax
from jax.experimental import pallas as pl
from jax.experimental.pallas import tpu as pltpu
from jax.sharding import PartitionSpec as P

BLADES = 4
NEIGHBORS = 6
RIM = 16
MESH = pl.DeviceIdType.MESH
CHUNK = 16


def derivative_entry(offset, instances):
    offset %= instances
    if offset == 0 or 2 * offset == instances:
        return 0.0
    return 0.5 * (-1.0) ** offset / math.tan(math.pi * offset / instances)


def fluxes(values):
    density = values[0]
    safe_density = jnp.where(density > 0, density, 1.0)
    momenta = values[1:4]
    energy = values[4]
    speeds = [m / safe_density for m in momenta]
    kinetic = momenta[0] * speeds[0] + momenta[1] * speeds[1] + momenta[2] * speeds[2]
    pressure = 0.4 * (energy - 0.5 * kinetic)
    result = []
    for direction in range(3):
        pieces = [momenta[direction]]
        for component in range(3):
            term = momenta[component] * speeds[direction]
            pieces.append(term + pressure if component == direction else term)
        pieces.append((energy + pressure) * speeds[direction])
        result.append(pieces)
    return result


def kernel(
    peers_inst, peers_dom, cells,
    flow_in, weight, adj_in, tile_in, row_in, partner_in, side_in, count_in, freq_in,
    out,
    flow, adj, face_tile, face_row, face_partner, face_side, count, freq,
    ubf, ain, tout, tin, stage, halo, wv, fp, ut, codes, pout, pmid, psum, pin, acc,
    in_sem, code_sem, halo_sem, a_sem, t_sem, m_sem, p_sem,
):
    n, ndom = peers_inst, peers_dom
    comps, tiles, width = flow.shape
    faces = face_tile.shape[1]
    slots = width // cells
    instances = n * slots
    lag = instances // BLADES // slots
    part = tiles // n
    ops = weight.shape[0]
    per_op = comps * cells
    aligned = part % CHUNK == 0
    rows = ubf.shape[1]
    wide = fp.shape[2] // slots
    shift = cells.bit_length() - 1
    me_i = lax.axis_index("inst")
    me_d = lax.axis_index("dom")

    def inst_at(step):
        return lax.rem(me_i + (step % n), n)

    def dom_at(step):
        return lax.rem(me_d + (step % ndom), ndom)

    def at(dom_step, inst_step):
        return {"inst": inst_at(inst_step), "dom": dom_at(dom_step)}

    def remote(src, dst, sems, index, target):
        return pltpu.make_async_remote_copy(
            src_ref=src,
            dst_ref=dst,
            send_sem=sems.at[(0,) + index],
            recv_sem=sems.at[(1,) + index],
            device_id=target,
            device_id_type=MESH,
        )

    partners = {(j, 0) for j in range(1, ndom)} | {(0, i) for i in range(1, n)}
    partners |= {(0, lag % n), (0, -lag % n)}
    partners = sorted(partners)
    barrier = pltpu.get_barrier_semaphore()
    for dom_step, inst_step in partners:
        pl.semaphore_signal(
            barrier, inc=1, device_id=at(dom_step, inst_step), device_id_type=MESH
        )
    arriving = [
        pltpu.make_async_copy(src, dst, in_sem.at[i])
        for i, (src, dst) in enumerate(
            (
                (flow_in, flow),
                (partner_in, face_partner),
                (row_in, face_row),
                (adj_in, adj),
                (tile_in, face_tile),
                (side_in, face_side),
                (count_in, count),
                (freq_in, freq),
                (weight, wv),
            )
        )
    ]
    for copy in arriving[:-1]:
        copy.start()
    flow_copy, partner_copy, row_copy, *other_copies, weight_copy = arriving

    flow_copy.wait()
    weight_copy.start()
    for p in range(n):
        if aligned:
            for c in range(comps):
                ubf[p, c * part : (c + 1) * part] = flow[
                    c, p * part : (p + 1) * part
                ].astype(jnp.bfloat16)
        else:
            stage[...] = jnp.zeros_like(stage)
            for c in range(comps):
                stage[c * part : (c + 1) * part] = flow[c, p * part : (p + 1) * part]
            ubf[p] = stage[...].astype(jnp.bfloat16)
    partner_copy.wait()
    row_copy.wait()
    code = face_partner[...] * cells + face_row[...]
    codes[0] = jnp.broadcast_to(code, (8, faces))
    pl.semaphore_wait(barrier, len(partners))

    code_copies = [
        remote(codes.at[0], codes.at[j], code_sem, (j,), at(j, 0)) for j in range(1, ndom)
    ]
    for copy in code_copies:
        copy.start()
    halves = 2 if rows % (2 * CHUNK) == 0 else 1
    half = rows // halves
    a_copies = [
        [
            remote(
                ubf.at[inst_at(i), pl.ds(h * half, half)],
                ain.at[i, pl.ds(h * half, half)],
                a_sem, (i, h), at(0, i),
            )
            for i in range(1, n)
        ]
        for h in range(halves)
    ]
    for group in a_copies:
        for copy in group:
            copy.start()
    halo_copies = [
        remote(flow_in.at[:, tiles - RIM :], halo.at[0], halo_sem, (0,), at(1, 0)),
        remote(flow_in.at[:, :RIM], halo.at[1], halo_sem, (1,), at(-1, 0)),
    ]
    for copy in halo_copies:
        copy.start()

    low_lanes = lax.broadcasted_iota(jnp.int32, (CHUNK, width), 1) < cells

    def swap(value):
        return pltpu.roll(value, cells, 1)

    def put_fluxes(read, base):
        for direction, pieces in enumerate(fluxes(read)):
            for pair in range((comps + 1) // 2):
                first = pieces[2 * pair]
                cols = slice(pair * width, (pair + 1) * width)
                more = slice(wide + pair * width, wide + (pair + 1) * width)
                if 2 * pair + 1 < comps:
                    second = pieces[2 * pair + 1]
                    left = jnp.where(low_lanes, first, swap(second))
                    right = jnp.where(low_lanes, swap(first), second)
                else:
                    left, right = first, swap(first)
                fp[direction, base : base + CHUNK, cols] = left.astype(jnp.bfloat16)
                fp[direction, base : base + CHUNK, more] = right.astype(jnp.bfloat16)

    for c in range(comps):
        ut[c * width : (c + 1) * width] = flow[c].T.astype(jnp.bfloat16)
    for t in range(0, tiles, CHUNK):
        put_fluxes([flow[c, t : t + CHUNK] for c in range(comps)], RIM + t)

    cell_ids = lax.broadcasted_iota(jnp.int32, (cells, faces), 0)
    tile_ids = lax.broadcasted_iota(jnp.int32, (tiles, faces), 0)
    m_copies = []
    for j in range(ndom):
        if j:
            code_copies[j - 1].wait_recv()
        wanted = codes[j][:1]
        wanted_tile = lax.shift_right_logical(wanted, shift) - me_d * tiles
        wanted_cell = lax.bitwise_and(wanted, cells - 1)
        pick = jnp.where(tile_ids == wanted_tile, 1.0, 0.0).astype(jnp.bfloat16)
        found = jnp.dot(ut[...], pick, preferred_element_type=jnp.float32)
        mask = cell_ids == wanted_cell
        lines = [
            jnp.sum(
                jnp.where(mask, found[g * cells : (g + 1) * cells], 0.0),
                axis=0,
                keepdims=True,
            )
            for g in range(comps * slots)
        ]
        lines.append(jnp.zeros((pout.shape[1] - comps * slots, faces), jnp.float32))
        found = jnp.concatenate(lines, axis=0).astype(jnp.bfloat16)
        if j == 0:
            pmid[0] = found
        else:
            pout[j] = found
            copy = remote(pout.at[j], pmid.at[j], m_sem, (j,), at(-j, 0))
            copy.start()
            m_copies.append(copy)

    cross = [
        jnp.where(
            low_lanes,
            derivative_entry(2 * delta - 1, instances),
            derivative_entry(2 * delta + 1, instances),
        ).astype(jnp.float32)
        for delta in range(n)
    ]
    t_copies = []
    p_copies = []
    for h in range(halves):
        for copy in a_copies[h]:
            copy.wait_recv()
        for r in range(h * half, (h + 1) * half, CHUNK):
            plain = [
                (ubf[me_i, r : r + CHUNK] if i == 0 else ain[i, r : r + CHUNK]).astype(
                    jnp.float32
                )
                for i in range(n)
            ]
            turned = [swap(value) for value in plain]
            for m in range(n):
                total = jnp.zeros((CHUNK, width), jnp.float32)
                for i in range(n):
                    even = derivative_entry(2 * (m + i), instances)
                    if even != 0.0:
                        total = total + even * plain[i]
                    total = total + cross[(m + i) % n] * turned[i]
                total = total.astype(jnp.bfloat16)
                if m == 0:
                    tin[me_i, r : r + CHUNK] = total
                else:
                    tout[m, r : r + CHUNK] = total
        group = [
            remote(
                tout.at[m, pl.ds(h * half, half)],
                tin.at[me_i, pl.ds(h * half, half)],
                t_sem, (m, h), at(0, m),
            )
            for m in range(1, n)
        ]
        for copy in group:
            copy.start()
        t_copies.append(group)
        if h == 0:
            for copy in m_copies:
                copy.wait_recv()
            known = pmid[0]
            for j in range(1, ndom):
                known = known + pmid[j]
            psum[...] = known
            for way, step in enumerate((-lag, lag)):
                copy = remote(psum, pin.at[way], p_sem, (way,), at(0, step))
                copy.start()
                p_copies.append(copy)

    for copy in other_copies:
        copy.wait()
    weight_copy.wait()

    def apply(left, right, op):
        w = wv[op]
        both = jnp.concatenate([left, right], axis=0)
        return jnp.dot(both, w, preferred_element_type=jnp.float32)

    total = None
    for direction in range(3):
        own = fp[direction, RIM : RIM + tiles]
        term = apply(own[:, :per_op], own[:, wide : wide + per_op], NEIGHBORS + direction)
        total = term if total is None else total + term

    for copy in halo_copies:
        copy.wait_recv()
    for side, base in ((0, 0), (1, RIM + tiles)):
        put_fluxes([halo[side, c] for c in range(comps)], base)
    neighbor_ids = lax.broadcasted_iota(jnp.int32, (tiles, tiles + 2 * RIM), 1)
    shifted = jnp.concatenate([adj[...], jnp.zeros((8 - NEIGHBORS, tiles), jnp.int32)], axis=0)
    shifted = shifted.T - (me_d * tiles - RIM)
    for direction in range(3):
        pick = jnp.concatenate(
            [
                jnp.where(shifted[:, s : s + 1] == neighbor_ids, 1.0, 0.0).astype(jnp.bfloat16)
                for s in (2 * direction, 2 * direction + 1)
            ],
            axis=0,
        )
        picked = jnp.dot(pick, fp[direction], preferred_element_type=jnp.float32)
        picked = picked.astype(jnp.bfloat16)
        for s in range(2):
            block = picked[s * tiles : (s + 1) * tiles]
            total = total + apply(
                block[:, :per_op], block[:, wide : wide + per_op], 2 * direction + s
            )
    acc[:, :per_op] = total

    side = face_side[...] == 1
    live = lax.broadcasted_iota(jnp.int32, (1, faces), 1) < count[0]
    own_tile = jnp.where(live, face_tile[...] - me_d * tiles, -1)
    place = jnp.where(tile_ids == own_tile, 1.0, 0.0).astype(jnp.bfloat16)
    mask = cell_ids == face_row[...]
    ones = jnp.where(mask, 1.0, 0.0).astype(jnp.bfloat16)
    contract = (((1,), (1,)), ((), ()))
    times = lax.dot_general(
        place, jnp.concatenate([ones] * slots, axis=0), contract,
        preferred_element_type=jnp.float32,
    )
    for copy in p_copies:
        copy.wait_recv()
    lagged = jnp.where(side, pin[0].astype(jnp.float32), pin[1].astype(jnp.float32))
    lines = [lagged[g : g + 1] for g in range(comps * slots)]
    cosine = math.cos(2.0 * math.pi / BLADES)
    sine = jnp.where(side, 1.0, -1.0) * math.sin(2.0 * math.pi / BLADES)
    for k in range(slots):
        m0, m1 = lines[slots + k], lines[2 * slots + k]
        lines[slots + k] = cosine * m0 - sine * m1
        lines[2 * slots + k] = sine * m0 + cosine * m1
    spread = jnp.concatenate(
        [jnp.where(mask, line, 0.0).astype(jnp.bfloat16) for line in lines], axis=0
    )
    gained = lax.dot_general(place, spread, contract, preferred_element_type=jnp.float32)

    for t in range(0, tiles, CHUNK):
        span = slice(t, t + CHUNK)
        more = slice(tiles + t, tiles + t + CHUNK)
        for c in range(comps):
            pair = c // 2
            cols = slice(pair * width, (pair + 1) * width)
            if c % 2 == 0:
                spatial = jnp.where(low_lanes, acc[span, cols], swap(acc[more, cols]))
            else:
                spatial = jnp.where(low_lanes, swap(acc[span, cols]), acc[more, cols])
            out[c, span] = (
                spatial
                + gained[span, c * width : (c + 1) * width]
                - times[span] * flow[c, span]
            )
    speed = freq[0]
    for m in range(n):
        if m:
            for group in t_copies:
                group[m - 1].wait_recv()
        p = inst_at(-m)
        if not aligned:
            stage[...] = tin[p].astype(jnp.float32)
        for c in range(comps):
            block = slice(c * part, (c + 1) * part)
            temporal = tin[p, block].astype(jnp.float32) if aligned else stage[block]
            if aligned:
                span = pl.ds(pl.multiple_of(p * part, part), part)
            else:
                span = pl.ds(p * part, part)
            out[c, span] = out[c, span] + speed * temporal

    flat = [copy for group in a_copies + t_copies for copy in group]
    for copy in code_copies + flat + halo_copies + m_copies + p_copies:
        copy.wait_send()


def body(
    n, ndom,
    flow_state, op_weight, adjacency, face_tile, face_row, face_partner, face_side,
    face_count, frequency,
):
    comps, tiles, width = flow_state.shape
    ops, per_op, _ = op_weight.shape
    cells = per_op // comps
    faces = face_tile.shape[0]
    slots = width // cells
    rows = -(-(comps * (tiles // n)) // CHUNK) * CHUNK
    wide = -(-comps // 2) * width
    packed = -(-(comps * slots) // 16) * 16
    in_vmem = pl.BlockSpec(memory_space=pltpu.VMEM)
    in_hbm = pl.BlockSpec(memory_space=pltpu.HBM)
    i32 = jnp.int32
    bf16, f32 = jnp.bfloat16, jnp.float32
    dma = pltpu.SemaphoreType.DMA
    line = lambda values: values.reshape(1, faces)
    return pl.pallas_call(
        functools.partial(kernel, n, ndom, cells),
        out_shape=jax.ShapeDtypeStruct(flow_state.shape, f32),
        in_specs=[in_hbm] * 9,
        out_specs=in_vmem,
        scratch_shapes=[
            pltpu.VMEM(flow_state.shape, f32),
            pltpu.VMEM((NEIGHBORS, tiles), i32),
            pltpu.VMEM((1, faces), i32),
            pltpu.VMEM((1, faces), i32),
            pltpu.VMEM((1, faces), i32),
            pltpu.VMEM((1, faces), i32),
            pltpu.SMEM((1,), i32),
            pltpu.SMEM((1,), f32),
            pltpu.VMEM((n, rows, width), bf16),
            pltpu.VMEM((n, rows, width), bf16),
            pltpu.VMEM((n, rows, width), bf16),
            pltpu.VMEM((n, rows, width), bf16),
            pltpu.VMEM((rows, width), f32),
            pltpu.VMEM((2, comps, RIM, width), f32),
            pltpu.VMEM(op_weight.shape, bf16),
            pltpu.VMEM((3, tiles + 2 * RIM, slots * wide), bf16),
            pltpu.VMEM((comps * width, tiles), bf16),
            pltpu.VMEM((ndom, 8, faces), jnp.int32),
            pltpu.VMEM((ndom, packed, faces), bf16),
            pltpu.VMEM((ndom, packed, faces), bf16),
            pltpu.VMEM((packed, faces), bf16),
            pltpu.VMEM((2, packed, faces), bf16),
            pltpu.VMEM((slots * tiles, wide), f32),
            dma((9,)),
            dma((2, ndom)),
            dma((2, 2)),
            dma((2, n, 2)),
            dma((2, n, 2)),
            dma((2, ndom)),
            dma((2, 2)),
        ],
        compiler_params=pltpu.CompilerParams(
            collective_id=0, has_side_effects=True, vmem_limit_bytes=64 * 1024 * 1024
        ),
    )(
        flow_state, op_weight, adjacency.T, line(face_tile), line(face_row),
        line(face_partner), line(face_side), face_count, frequency,
    )


def solution(mesh):
    placed = (
        P("groups", "dom", "inst"),
        P(),
        P("dom", None),
        P("dom"),
        P("dom"),
        P("dom"),
        P("dom"),
        P("dom"),
        P("groups"),
    )
    return jax.shard_map(
        functools.partial(body, mesh.shape["inst"], mesh.shape["dom"]),
        mesh=mesh,
        in_specs=placed,
        out_specs=P("groups", "dom", "inst"),
        check_vma=False,
    )
```

```python
import functools
import math

import jax
import jax.numpy as jnp
from jax import lax
from jax.experimental import pallas as pl
from jax.experimental.pallas import tpu as pltpu
from jax.sharding import PartitionSpec as P

BLADES = 4
NEIGHBORS = 6
RIM = 16
MESH = pl.DeviceIdType.MESH
CHUNK = 16


def derivative_entry(offset, instances):
    offset %= instances
    if offset == 0 or 2 * offset == instances:
        return 0.0
    return 0.5 * (-1.0) ** offset / math.tan(math.pi * offset / instances)


def fluxes(values):
    density = values[0]
    safe_density = jnp.where(density > 0, density, 1.0)
    momenta = values[1:4]
    energy = values[4]
    speeds = [m / safe_density for m in momenta]
    kinetic = momenta[0] * speeds[0] + momenta[1] * speeds[1] + momenta[2] * speeds[2]
    pressure = 0.4 * (energy - 0.5 * kinetic)
    result = []
    for direction in range(3):
        pieces = [momenta[direction]]
        for component in range(3):
            term = momenta[component] * speeds[direction]
            pieces.append(term + pressure if component == direction else term)
        pieces.append((energy + pressure) * speeds[direction])
        result.append(pieces)
    return result


def kernel(
    peers_inst, peers_dom, cells,
    flow_in, weight, adj_in, tile_in, row_in, partner_in, side_in, count_in,
    base_out, tin,
    flow, adj, face_tile, face_row, face_partner, face_side, count,
    out, ubf, ain, tout, stage, halo, wv, fp, ut, codes, pout, pmid, psum, pin, acc,
    in_sem, code_sem, halo_sem, a_sem, t_sem, m_sem, p_sem, out_sem,
):
    n, ndom = peers_inst, peers_dom
    comps, tiles, width = flow.shape
    faces = face_tile.shape[1]
    slots = width // cells
    instances = n * slots
    lag = instances // BLADES // slots
    part = tiles // n
    ops = weight.shape[0]
    per_op = comps * cells
    aligned = part % CHUNK == 0
    rows = ubf.shape[1]
    wide = fp.shape[2] // slots
    shift = cells.bit_length() - 1
    me_i = lax.axis_index("inst")
    me_d = lax.axis_index("dom")

    def inst_at(step):
        return lax.rem(me_i + (step % n), n)

    def dom_at(step):
        return lax.rem(me_d + (step % ndom), ndom)

    def at(dom_step, inst_step):
        return {"inst": inst_at(inst_step), "dom": dom_at(dom_step)}

    def remote(src, dst, sems, index, target):
        return pltpu.make_async_remote_copy(
            src_ref=src,
            dst_ref=dst,
            send_sem=sems.at[(0,) + index],
            recv_sem=sems.at[(1,) + index],
            device_id=target,
            device_id_type=MESH,
        )

    partners = {(j, 0) for j in range(1, ndom)} | {(0, i) for i in range(1, n)}
    partners |= {(0, lag % n), (0, -lag % n)}
    partners = sorted(partners)
    barrier = pltpu.get_barrier_semaphore()
    for dom_step, inst_step in partners:
        pl.semaphore_signal(
            barrier, inc=1, device_id=at(dom_step, inst_step), device_id_type=MESH
        )
    arriving = [
        pltpu.make_async_copy(src, dst, in_sem.at[i])
        for i, (src, dst) in enumerate(
            (
                (flow_in, flow),
                (partner_in, face_partner),
                (row_in, face_row),
                (adj_in, adj),
                (tile_in, face_tile),
                (side_in, face_side),
                (count_in, count),
                (weight, wv),
            )
        )
    ]
    for copy in arriving[:-1]:
        copy.start()
    flow_copy, partner_copy, row_copy, *other_copies, weight_copy = arriving

    flow_copy.wait()
    weight_copy.start()
    for p in range(n):
        if aligned:
            for c in range(comps):
                ubf[p, c * part : (c + 1) * part] = flow[
                    c, p * part : (p + 1) * part
                ].astype(jnp.bfloat16)
        else:
            stage[...] = jnp.zeros_like(stage)
            for c in range(comps):
                stage[c * part : (c + 1) * part] = flow[c, p * part : (p + 1) * part]
            ubf[p] = stage[...].astype(jnp.bfloat16)
    partner_copy.wait()
    row_copy.wait()
    code = face_partner[...] * cells + face_row[...]
    codes[0] = jnp.broadcast_to(code, (8, faces))
    pl.semaphore_wait(barrier, len(partners))

    code_copies = [
        remote(codes.at[0], codes.at[j], code_sem, (j,), at(j, 0)) for j in range(1, ndom)
    ]
    for copy in code_copies:
        copy.start()
    halves = 2 if rows % (2 * CHUNK) == 0 else 1
    half = rows // halves
    a_copies = [
        [
            remote(
                ubf.at[inst_at(i), pl.ds(h * half, half)],
                ain.at[i, pl.ds(h * half, half)],
                a_sem, (i, h), at(0, i),
            )
            for i in range(1, n)
        ]
        for h in range(halves)
    ]
    for group in a_copies:
        for copy in group:
            copy.start()
    halo_copies = [
        remote(flow_in.at[:, tiles - RIM :], halo.at[0], halo_sem, (0,), at(1, 0)),
        remote(flow_in.at[:, :RIM], halo.at[1], halo_sem, (1,), at(-1, 0)),
    ]
    for copy in halo_copies:
        copy.start()

    low_lanes = lax.broadcasted_iota(jnp.int32, (CHUNK, width), 1) < cells

    def swap(value):
        return pltpu.roll(value, cells, 1)

    def put_fluxes(read, base):
        for direction, pieces in enumerate(fluxes(read)):
            for pair in range((comps + 1) // 2):
                first = pieces[2 * pair]
                cols = slice(pair * width, (pair + 1) * width)
                more = slice(wide + pair * width, wide + (pair + 1) * width)
                if 2 * pair + 1 < comps:
                    second = pieces[2 * pair + 1]
                    left = jnp.where(low_lanes, first, swap(second))
                    right = jnp.where(low_lanes, swap(first), second)
                else:
                    left, right = first, swap(first)
                fp[direction, base : base + CHUNK, cols] = left.astype(jnp.bfloat16)
                fp[direction, base : base + CHUNK, more] = right.astype(jnp.bfloat16)

    for c in range(comps):
        ut[c * width : (c + 1) * width] = flow[c].T.astype(jnp.bfloat16)
    for t in range(0, tiles, CHUNK):
        put_fluxes([flow[c, t : t + CHUNK] for c in range(comps)], RIM + t)

    cell_ids = lax.broadcasted_iota(jnp.int32, (cells, faces), 0)
    tile_ids = lax.broadcasted_iota(jnp.int32, (tiles, faces), 0)
    m_copies = []
    for j in range(ndom):
        if j:
            code_copies[j - 1].wait_recv()
        wanted = codes[j][:1]
        wanted_tile = lax.shift_right_logical(wanted, shift) - me_d * tiles
        wanted_cell = lax.bitwise_and(wanted, cells - 1)
        pick = jnp.where(tile_ids == wanted_tile, 1.0, 0.0).astype(jnp.bfloat16)
        found = jnp.dot(ut[...], pick, preferred_element_type=jnp.float32)
        mask = cell_ids == wanted_cell
        lines = [
            jnp.sum(
                jnp.where(mask, found[g * cells : (g + 1) * cells], 0.0),
                axis=0,
                keepdims=True,
            )
            for g in range(comps * slots)
        ]
        lines.append(jnp.zeros((pout.shape[1] - comps * slots, faces), jnp.float32))
        found = jnp.concatenate(lines, axis=0).astype(jnp.bfloat16)
        if j == 0:
            pmid[0] = found
        else:
            pout[j] = found
            copy = remote(pout.at[j], pmid.at[j], m_sem, (j,), at(-j, 0))
            copy.start()
            m_copies.append(copy)

    cross = [
        jnp.where(
            low_lanes,
            derivative_entry(2 * delta - 1, instances),
            derivative_entry(2 * delta + 1, instances),
        ).astype(jnp.float32)
        for delta in range(n)
    ]
    t_copies = []
    p_copies = []
    leaving = []
    for h in range(halves):
        for copy in a_copies[h]:
            copy.wait_recv()
        for r in range(h * half, (h + 1) * half, CHUNK):
            plain = [
                (ubf[me_i, r : r + CHUNK] if i == 0 else ain[i, r : r + CHUNK]).astype(
                    jnp.float32
                )
                for i in range(n)
            ]
            turned = [swap(value) for value in plain]
            for m in range(n):
                total = jnp.zeros((CHUNK, width), jnp.float32)
                for i in range(n):
                    even = derivative_entry(2 * (m + i), instances)
                    if even != 0.0:
                        total = total + even * plain[i]
                    total = total + cross[(m + i) % n] * turned[i]
                total = total.astype(jnp.bfloat16)
                tout[m, r : r + CHUNK] = total
        group = [
            remote(
                tout.at[m, pl.ds(h * half, half)],
                tin.at[me_i, pl.ds(h * half, half)],
                t_sem, (m, h), at(0, m),
            )
            for m in range(1, n)
        ]
        for copy in group:
            copy.start()
        t_copies.append(group)
        own_copy = pltpu.make_async_copy(
            tout.at[0, pl.ds(h * half, half)],
            tin.at[me_i, pl.ds(h * half, half)],
            out_sem.at[1 + h],
        )
        own_copy.start()
        leaving.append(own_copy)
        if h == 0:
            for copy in m_copies:
                copy.wait_recv()
            known = pmid[0]
            for j in range(1, ndom):
                known = known + pmid[j]
            psum[...] = known
            for way, step in enumerate((-lag, lag)):
                copy = remote(psum, pin.at[way], p_sem, (way,), at(0, step))
                copy.start()
                p_copies.append(copy)

    for copy in other_copies:
        copy.wait()
    weight_copy.wait()

    def apply(left, right, op):
        w = wv[op]
        both = jnp.concatenate([left, right], axis=0)
        return jnp.dot(both, w, preferred_element_type=jnp.float32)

    total = None
    for direction in range(3):
        own = fp[direction, RIM : RIM + tiles]
        term = apply(own[:, :per_op], own[:, wide : wide + per_op], NEIGHBORS + direction)
        total = term if total is None else total + term

    for copy in halo_copies:
        copy.wait_recv()
    for side, base in ((0, 0), (1, RIM + tiles)):
        put_fluxes([halo[side, c] for c in range(comps)], base)
    neighbor_ids = lax.broadcasted_iota(jnp.int32, (tiles, tiles + 2 * RIM), 1)
    shifted = jnp.concatenate([adj[...], jnp.zeros((8 - NEIGHBORS, tiles), jnp.int32)], axis=0)
    shifted = shifted.T - (me_d * tiles - RIM)
    for direction in range(3):
        pick = jnp.concatenate(
            [
                jnp.where(shifted[:, s : s + 1] == neighbor_ids, 1.0, 0.0).astype(jnp.bfloat16)
                for s in (2 * direction, 2 * direction + 1)
            ],
            axis=0,
        )
        picked = jnp.dot(pick, fp[direction], preferred_element_type=jnp.float32)
        picked = picked.astype(jnp.bfloat16)
        for s in range(2):
            block = picked[s * tiles : (s + 1) * tiles]
            total = total + apply(
                block[:, :per_op], block[:, wide : wide + per_op], 2 * direction + s
            )
    acc[:, :per_op] = total

    side = face_side[...] == 1
    live = lax.broadcasted_iota(jnp.int32, (1, faces), 1) < count[0]
    own_tile = jnp.where(live, face_tile[...] - me_d * tiles, -1)
    place = jnp.where(tile_ids == own_tile, 1.0, 0.0).astype(jnp.bfloat16)
    mask = cell_ids == face_row[...]
    ones = jnp.where(mask, 1.0, 0.0).astype(jnp.bfloat16)
    contract = (((1,), (1,)), ((), ()))
    times = lax.dot_general(
        place, jnp.concatenate([ones] * slots, axis=0), contract,
        preferred_element_type=jnp.float32,
    )
    for copy in p_copies:
        copy.wait_recv()
    lagged = jnp.where(side, pin[0].astype(jnp.float32), pin[1].astype(jnp.float32))
    lines = [lagged[g : g + 1] for g in range(comps * slots)]
    cosine = math.cos(2.0 * math.pi / BLADES)
    sine = jnp.where(side, 1.0, -1.0) * math.sin(2.0 * math.pi / BLADES)
    for k in range(slots):
        m0, m1 = lines[slots + k], lines[2 * slots + k]
        lines[slots + k] = cosine * m0 - sine * m1
        lines[2 * slots + k] = sine * m0 + cosine * m1
    spread = jnp.concatenate(
        [jnp.where(mask, line, 0.0).astype(jnp.bfloat16) for line in lines], axis=0
    )
    gained = lax.dot_general(place, spread, contract, preferred_element_type=jnp.float32)

    for t in range(0, tiles, CHUNK):
        span = slice(t, t + CHUNK)
        more = slice(tiles + t, tiles + t + CHUNK)
        for c in range(comps):
            pair = c // 2
            cols = slice(pair * width, (pair + 1) * width)
            if c % 2 == 0:
                spatial = jnp.where(low_lanes, acc[span, cols], swap(acc[more, cols]))
            else:
                spatial = jnp.where(low_lanes, swap(acc[span, cols]), acc[more, cols])
            out[c, span] = (
                spatial
                + gained[span, c * width : (c + 1) * width]
                - times[span] * flow[c, span]
            )
    base_copy = pltpu.make_async_copy(out, base_out, out_sem.at[0])
    base_copy.start()
    for group in t_copies:
        for copy in group:
            copy.wait_recv()
    for copy in leaving + [base_copy]:
        copy.wait()

    flat = [copy for group in a_copies + t_copies for copy in group]
    for copy in code_copies + flat + halo_copies + m_copies + p_copies:
        copy.wait_send()


def finish(base_in, tin_in, freq, out, base, tin, stage, sems):
    comps, tiles, _ = base.shape
    n, _, _ = tin.shape
    part = tiles // n
    aligned = part % CHUNK == 0
    tin_copy = pltpu.make_async_copy(tin_in, tin, sems.at[2 * comps])
    tin_copy.start()
    copies = [
        pltpu.make_async_copy(base_in.at[c], base.at[c], sems.at[c]) for c in range(comps)
    ]
    for copy in copies:
        copy.start()
    leaving = [
        pltpu.make_async_copy(base.at[c], out.at[c], sems.at[comps + c]) for c in range(comps)
    ]
    tin_copy.wait()
    speed = freq[0]
    for c in range(comps):
        copies[c].wait()
        for p in range(n):
            span = slice(p * part, (p + 1) * part)
            block = slice(c * part, (c + 1) * part)
            if aligned:
                temporal = tin[p, block].astype(jnp.float32)
            else:
                stage[...] = tin[p].astype(jnp.float32)
                temporal = stage[block]
            base[c, span] = base[c, span] + speed * temporal
        leaving[c].start()
    for copy in leaving:
        copy.wait()


def body(
    n, ndom,
    flow_state, op_weight, adjacency, face_tile, face_row, face_partner, face_side,
    face_count, frequency,
):
    comps, tiles, width = flow_state.shape
    ops, per_op, _ = op_weight.shape
    cells = per_op // comps
    faces = face_tile.shape[0]
    slots = width // cells
    rows = -(-(comps * (tiles // n)) // CHUNK) * CHUNK
    wide = -(-comps // 2) * width
    packed = -(-(comps * slots) // 16) * 16
    in_hbm = pl.BlockSpec(memory_space=pltpu.HBM)
    i32 = jnp.int32
    bf16, f32 = jnp.bfloat16, jnp.float32
    dma = pltpu.SemaphoreType.DMA
    line = lambda values: values.reshape(1, faces)
    derived = (n, rows, width)
    base, tin = pl.pallas_call(
        functools.partial(kernel, n, ndom, cells),
        out_shape=(
            jax.ShapeDtypeStruct(flow_state.shape, f32),
            jax.ShapeDtypeStruct(derived, bf16),
        ),
        in_specs=[in_hbm] * 8,
        out_specs=(in_hbm, in_hbm),
        scratch_shapes=[
            pltpu.VMEM(flow_state.shape, f32),
            pltpu.VMEM((NEIGHBORS, tiles), i32),
            pltpu.VMEM((1, faces), i32),
            pltpu.VMEM((1, faces), i32),
            pltpu.VMEM((1, faces), i32),
            pltpu.VMEM((1, faces), i32),
            pltpu.SMEM((1,), i32),
            pltpu.VMEM(flow_state.shape, f32),
            pltpu.VMEM(derived, bf16),
            pltpu.VMEM(derived, bf16),
            pltpu.VMEM(derived, bf16),
            pltpu.VMEM((rows, width), f32),
            pltpu.VMEM((2, comps, RIM, width), f32),
            pltpu.VMEM(op_weight.shape, bf16),
            pltpu.VMEM((3, tiles + 2 * RIM, slots * wide), bf16),
            pltpu.VMEM((comps * width, tiles), bf16),
            pltpu.VMEM((ndom, 8, faces), jnp.int32),
            pltpu.VMEM((ndom, packed, faces), bf16),
            pltpu.VMEM((ndom, packed, faces), bf16),
            pltpu.VMEM((packed, faces), bf16),
            pltpu.VMEM((2, packed, faces), bf16),
            pltpu.VMEM((slots * tiles, wide), f32),
            dma((8,)),
            dma((2, ndom)),
            dma((2, 2)),
            dma((2, n, 2)),
            dma((2, n, 2)),
            dma((2, ndom)),
            dma((2, 2)),
            dma((3,)),
        ],
        compiler_params=pltpu.CompilerParams(
            collective_id=0, has_side_effects=True, vmem_limit_bytes=64 * 1024 * 1024
        ),
    )(
        flow_state, op_weight, adjacency.T, line(face_tile), line(face_row),
        line(face_partner), line(face_side), face_count,
    )
    return pl.pallas_call(
        finish,
        out_shape=jax.ShapeDtypeStruct(base.shape, f32),
        in_specs=[in_hbm, in_hbm, pl.BlockSpec(memory_space=pltpu.SMEM)],
        out_specs=in_hbm,
        scratch_shapes=[
            pltpu.VMEM(base.shape, f32),
            pltpu.VMEM(derived, bf16),
            pltpu.VMEM((rows, width), f32),
            dma((2 * comps + 1,)),
        ],
        compiler_params=pltpu.CompilerParams(vmem_limit_bytes=64 * 1024 * 1024),
    )(base, tin, frequency)


def solution(mesh):
    placed = (
        P("groups", "dom", "inst"),
        P(),
        P("dom", None),
        P("dom"),
        P("dom"),
        P("dom"),
        P("dom"),
        P("dom"),
        P("groups"),
    )
    return jax.shard_map(
        functools.partial(body, mesh.shape["inst"], mesh.shape["dom"]),
        mesh=mesh,
        in_specs=placed,
        out_specs=P("groups", "dom", "inst"),
        check_vma=False,
    )
```
